128 devices in a mesh: dp: 8 (over x, core), token: 16 (over z, y).
Axes of the slice: x: 4, y: 4, z: 4, core: 2. Of those that a mesh axis runs over, the one named last changes fastest.
Arguments:
- dense_tokens: bfloat16 [2048, 15, 768], P(('dp', 'token')), may hold values from -6 to 6
- cold_table: bfloat16 [131072, 128], P('dp'), may hold values from -6 to 6
- cold_ids: int32 [2048, 6, 16], P(('dp', 'token')), may hold values from 0 to 131071
- routes: int32 [16, 2048, 2], P(None, ('dp', 'token')), may hold values from 0 to 7, all different within a row; in each aligned block of 16 rows (0 to 15, 16 to 31, ..., all dimensions but the last counted through in order) at most 8 rows name the same one
- router: bfloat16 [16, 768, 8], replicated, may hold values from -0.21875 to 0.21875
- w_in: bfloat16 [16, 8, 768, 3072], P('token', 'dp'), may hold values from -0.21875 to 0.21875
- w_out: bfloat16 [16, 8, 3072, 768], P('token', 'dp'), may hold values from -0.109375 to 0.109375
Outputs:
- block_out: bfloat16 [2048, 16, 768], P(('dp', 'token'))
The draws below stay inside these ranges and needn't reach their ends.
Inputs may be any that keep to these rules, and one draw needn't show every extreme that they name: `routes`: the two experts of a row differ. In each aligned block of 16 rows along the samples (one device's samples for one token) no expert is named by more than 8 rows.
All inputs are finite; a program needn't handle non-finite values.
Results may differ from the reference program's by a relative error of at most 0.01.
Values may be sent and summed in bfloat16 or wider, within the bound.
A program may use at most 64 MiB of HBM per device.

```python
import math
import jax
import jax.numpy as jnp
import numpy as np
from jax import lax

D = 768
HID = 3072
NTOK = 16
EMB = 128
TOPK = 2
LISTLEN = 16
SMP_DEV = 16
EXPERTS = 8
GROUPS = 6
SAMPLES = 2048
ROWS = 131072
CAP = 8


def set_ends(values, key, least, top_value):
    extent = values.shape
    index_at = [jax.random.randint(jax.random.fold_in(key, axis), (), 0, extent[axis]) for axis in range(len(extent))]
    values = values.at[tuple(index_at)].set(least)
    longest = extent.index(max(extent))
    index_at[longest] = (index_at[longest] + 1) % extent[longest]
    return values.at[tuple(index_at)].set(top_value)


def shard_levels(own_key, dims, cuts, least, top_value):
    def one(dim, shards_of):
        heights = jax.random.uniform(jax.random.fold_in(jax.random.fold_in(own_key, 6), dim), (shards_of,), jnp.float32, least / len(cuts), top_value / len(cuts))
        return jnp.repeat(jnp.exp(heights), dims[dim] // shards_of).reshape((-1,) + (1,) * (len(dims) - dim - 1))

    loudness = one(*cuts[0])
    for cut in cuts[1:]:
        loudness = loudness * one(*cut)
    return loudness


def wide_ids(key, dims, number_of, skew):
    weights = [min(1 << octave, number_of + 1 - (1 << octave)) * (1 << 20) // math.isqrt((1 << octave) ** skew) + 1 for octave in range((number_of + 1).bit_length()) if 1 << octave <= number_of]
    scale = 1 + sum(weights) // (1 << 30)
    listing = np.cumsum(np.array([max(1, weight // scale) for weight in weights]))
    pick = jax.random.randint(jax.random.fold_in(key, 1), dims, 0, int(listing[len(weights) - 1]))
    start = jnp.left_shift(1, jnp.searchsorted(jnp.asarray(listing, jnp.int32), pick, side="right").astype(jnp.int32))
    standing = start - 1 + jax.random.randint(jax.random.fold_in(key, 4), dims, 0, 1 << 30) % jnp.minimum(start, number_of + 1 - start)
    return jax.random.permutation(jax.random.fold_in(key, 2), number_of)[standing].astype(jnp.int32)


def deal_out(own_key, own, number, rows, number_of, top, most, skew):
    ranking = jax.random.permutation(own_key, number_of)
    crowded, common = portions_of(number_of, rows * top, most, skew, True), portions_of(number_of, rows * top, most, skew, False)
    places = jnp.arange(number_of)

    def named(sizes, offset_by):
        used = int((sizes > 0).sum())
        fixed = max(1, used // 4)
        passed = fixed + (places - fixed + offset_by * (used - fixed)) % max(1, number_of - fixed)
        return jnp.zeros((number_of,), jnp.int32).at[ranking[jnp.where(places < fixed, places, passed)]].set(jnp.asarray(sizes, jnp.int32))

    sizes = jnp.where(number % 4 == 0, named(crowded, number // 4), named(common, number - number // 4 - 1))
    mixed = jax.random.permutation(jax.random.fold_in(own, 3), number_of)
    giver, sink = mixed[0:number_of // 2 * 2:2], mixed[1:number_of // 2 * 2:2]
    room = jnp.minimum(sizes[giver] - 1, most - sizes[sink]) // 2
    room = jnp.where((giver == ranking[0]) | (sink == ranking[0]) | (sizes[sink] == 0), 0, jnp.maximum(room, 0))
    passed = jax.random.randint(jax.random.fold_in(own, 4), (number_of // 2,), 0, 1 << 20) % (room + 1)
    sizes = sizes.at[giver].add(-passed).at[sink].add(passed)
    labels = jnp.searchsorted(jnp.cumsum(sizes), jnp.arange(rows * top), side="right").astype(jnp.int32)
    listing = labels.reshape(top, rows).T
    listing = listing[jax.random.permutation(jax.random.fold_in(own, 1), rows)]
    offset_by = jax.random.randint(jax.random.fold_in(own, 2), (rows, 1), 0, top)
    return jnp.take_along_axis(listing, (jnp.arange(top)[None, :] + offset_by) % top, axis=1)


def portions_of(amount, total, bound, skew, full):
    portions = [(1 << 20) // math.isqrt(rank ** skew) + 1 for rank in range(1, amount + 1)]
    largest = bound if full else min(bound, max(-(-total // amount), total * portions[0] // sum(portions)))
    least = 1 if total - largest >= amount - 1 else 0
    given, rest = [largest] + [least] * (amount - 1), total - largest - least * (amount - 1)
    while rest > 0:
        free = [i for i in range(1, amount) if given[i] < largest] or [i for i in range(1, amount) if given[i] < bound]
        mass, remaining = sum([portions[i] for i in free]), rest
        for i in free:
            addition = min(bound - given[i], max(1, remaining * portions[i] // mass), rest)
            given[i] = given[i] + addition
            rest = rest - addition
    return np.array(given)


def scatter_about(stream_key, shape, scale, limit, pieces=(), kind=jnp.bfloat16):
    factor_of = shard_levels(stream_key, shape, pieces, -0.22, 0.18) if pieces else 1.0
    values = jax.random.normal(stream_key, shape, jnp.float32) * scale * factor_of
    return jnp.minimum(jnp.maximum(values, -limit), limit).astype(kind)


def setup_inputs(seed: int = 0) -> dict:
    seeds = jax.random.split(jax.random.key(seed), 8)
    dense_tokens = scatter_about(seeds[0], (SAMPLES, NTOK - 1, D), 1.0, 6.0, ((0, 128),))
    cold_table = scatter_about(seeds[1], (ROWS, EMB), 1.0, 6.0, ((0, 8),))
    cold_ids = set_ends(wide_ids(seeds[2], (SAMPLES, GROUPS, LISTLEN), ROWS, 2), jax.random.fold_in(seeds[2], 3), 0, ROWS - 1).astype(jnp.int32)
    routes_keys = jax.random.split(jax.random.fold_in(seeds[3], 1), NTOK * SAMPLES // SMP_DEV)
    routes_turns = jax.random.permutation(jax.random.fold_in(seeds[3], 3), NTOK * SAMPLES // SMP_DEV)
    routes = jax.vmap(lambda own, number: deal_out(jax.random.fold_in(seeds[3], 2), own, number, SMP_DEV, EXPERTS, TOPK, CAP, 2))(routes_keys, routes_turns).reshape((NTOK, SAMPLES, TOPK))
    router = scatter_about(seeds[4], (NTOK, D, EXPERTS), D ** -0.5, 0.21875)
    w_in = scatter_about(seeds[5], (NTOK, EXPERTS, D, HID), D ** -0.5, 0.21875, ((0, 16), (1, 8)))
    w_out = scatter_about(seeds[6], (NTOK, EXPERTS, HID, D), HID ** -0.5, 0.109375, ((0, 16), (1, 8)))
    return {"dense_tokens": dense_tokens, "cold_table": cold_table, "cold_ids": cold_ids, "routes": routes, "router": router, "w_in": w_in, "w_out": w_out}


def layer_norm(value):
    mean = lax.optimization_barrier(jnp.mean(value, axis=-1, keepdims=True))
    centred = value - mean
    var = lax.optimization_barrier(jnp.mean(centred * centred, axis=-1, keepdims=True))
    return centred * lax.rsqrt(var + 1e-05)

def reference(dense_tokens, cold_table, cold_ids, routes, router, w_in, w_out):
    samples = dense_tokens.shape[0]
    width = dense_tokens.shape[2]
    ntok = router.shape[0]
    experts = router.shape[2]
    topk = routes.shape[2]
    length = cold_ids.shape[2]
    found = jnp.take(cold_table, cold_ids, axis=0).astype(jnp.float32)
    cold = (lax.optimization_barrier(jnp.sum(found, axis=2)) * (1.0 / math.sqrt(length))).reshape(samples, width)
    features = jnp.concatenate([dense_tokens.astype(jnp.float32), cold[:, None, :]], axis=1)
    head = width // ntok
    mixed = features.reshape(samples, ntok, ntok, head).transpose(0, 2, 1, 3).reshape(samples, ntok, width)
    normed = layer_norm(mixed + features).astype(jnp.bfloat16)
    by_token = normed.transpose(1, 0, 2)
    logits = jnp.einsum('tsd,tde->tse', by_token.astype(jnp.float32), router.astype(jnp.float32))
    picks = (routes[..., None] == jnp.arange(experts, dtype=jnp.int32)).astype(jnp.float32)
    gate = jax.nn.sigmoid(lax.optimization_barrier(jnp.sum(picks * logits[:, :, None, :], axis=-1)))
    global_cap = samples // SMP_DEV * CAP

    def per_token(items):
        rows, route, first, second = items
        onehot = (route.reshape(-1)[:, None] == jnp.arange(experts, dtype=jnp.int32)).astype(jnp.int32)
        position = lax.optimization_barrier(jnp.sum(jnp.cumsum(onehot, axis=0) * onehot, axis=-1)) - 1
        target = (route.reshape(-1) * global_cap + position).astype(jnp.int32)
        slot_rows = (jnp.arange(samples * topk, dtype=jnp.int32) // topk).astype(jnp.int32)
        source = jnp.zeros((experts * global_cap,), jnp.int32).at[target].set(slot_rows)
        filled = jnp.zeros((experts * global_cap,), jnp.bool_).at[target].set(True)
        bucket = jnp.where(filled[:, None], rows[source], jnp.zeros((), jnp.bfloat16))
        bucket = bucket.reshape(experts, global_cap, width)
        hidden = jnp.einsum('ecd,edh->ech', bucket.astype(jnp.float32), first.astype(jnp.float32))
        hidden = jax.nn.gelu(hidden, approximate=False).astype(jnp.bfloat16)
        output = jnp.einsum('ech,ehd->ecd', hidden.astype(jnp.float32), second.astype(jnp.float32)).astype(jnp.bfloat16)
        return output.reshape(experts * global_cap, width)[target].reshape(samples, topk, width)
    answers = lax.map(per_token, (by_token, routes, w_in, w_out))
    moe = lax.optimization_barrier(jnp.sum(gate[..., None] * answers.astype(jnp.float32), axis=2))
    result = layer_norm(by_token.astype(jnp.float32) + moe).astype(jnp.bfloat16)
    return result.transpose(1, 0, 2)
```

```python
import functools
import math

import jax
import jax.numpy as jnp
from jax import lax
from jax.experimental import pallas as pl
from jax.experimental.pallas import tpu as pltpu
from jax.sharding import PartitionSpec as P

CHUNKS = 4
PER = 32
CAP = 8
MESH = pl.DeviceIdType.MESH


def offsets(r):
    chunk, within = r // PER, r % PER
    dz, place = within // 8, within % 8
    return place // 2, place % 2, dz, (chunk + 4 - dz) % 4


def target_of(r, dp, tk):
    dx, dc, dz, dy = offsets(r)
    return (
        ((dp // 2 + dx) % 4) * 2 + (dp % 2 + dc) % 2,
        ((tk // 4 + dz) % 4) * 4 + (tk % 4 + dy) % 4,
    )


def source_of(r, dp, tk):
    dx, dc, dz, dy = offsets(r)
    return (
        ((dp // 2 + 4 - dx) % 4) * 2 + (dp % 2 + dc) % 2,
        ((tk // 4 + 4 - dz) % 4) * 4 + (tk % 4 + 4 - dy) % 4,
    )


def layer_norm(value):
    mean = jnp.mean(value, axis=-1, keepdims=True)
    centred = value - mean
    var = jnp.mean(centred * centred, axis=-1, keepdims=True)
    return centred * lax.rsqrt(var + 1e-05)


def gelu(value):
    return 0.5 * value * (1.0 + lax.erf(value * math.sqrt(0.5)))


def block_kernel(
    dense_ref, cold_ref, routes_ref, router_ref, w1_hbm, w2_hbm, out_ref,
    w1, w2, send, recv, back_send, back, slots, normed,
    w_sem, send_sem, recv_sem, back_send_sem, back_sem,
):
    dp, tk = lax.axis_index("dp"), lax.axis_index("token")
    mine = tk * 8 + dp
    load1 = pltpu.make_async_copy(w1_hbm, w1, w_sem.at[0])
    load2 = pltpu.make_async_copy(w2_hbm, w2, w_sem.at[1])
    load1.start()
    load2.start()
    barrier = pltpu.get_barrier_semaphore()

    def greet(r, carry):
        pl.semaphore_signal(barrier, inc=1, device_id=target_of(r, dp, tk), device_id_type=MESH)
        return carry

    lax.fori_loop(1, CHUNKS * PER, greet, 0)

    expert = lax.broadcasted_iota(jnp.int32, (16, 8, 32), 1)
    picks = (routes_ref[:, 0:1, :] == expert) | (routes_ref[:, 1:2, :] == expert)
    row = lax.broadcasted_iota(jnp.int32, (32, 32), 0)
    col = lax.broadcasted_iota(jnp.int32, (32, 32), 1)
    before = jnp.where((row // 16 == col // 16) & (row < col), 1.0, 0.0).astype(jnp.bfloat16)
    ones = jnp.where(picks, 1.0, 0.0)
    place = jnp.dot(
        ones.reshape(128, 32).astype(jnp.bfloat16), before, preferred_element_type=jnp.float32
    ).reshape(16, 8, 32)
    place = jnp.where(picks, place, -1.0)
    slot = lax.broadcasted_iota(jnp.int32, (16, 16, 32), 1)
    half = lax.broadcasted_iota(jnp.int32, (16, 16, 32), 2) // 16
    number = jnp.where(slot // 8 == half, slot % 8, -2).astype(jnp.float32)
    for e in range(8):
        slots[:, e * 16:(e + 1) * 16, :] = jnp.where(
            place[:, e:e + 1, :] == number, 1.0, 0.0
        ).astype(jnp.bfloat16)

    features = [dense_ref[t] for t in range(15)] + [cold_ref[...]]
    for h in range(16):
        mixed = jnp.concatenate([f[:, h * 48:(h + 1) * 48] for f in features], axis=1)
        rows = layer_norm(mixed.astype(jnp.float32) + features[h].astype(jnp.float32))
        rows = rows.astype(jnp.bfloat16)
        normed[h] = rows
        halves = jnp.concatenate([rows[:, :384], rows[:, 384:]], axis=0)
        out = jnp.dot(slots[h], halves, preferred_element_type=jnp.float32)
        send[h * 8:(h + 1) * 8] = out.astype(jnp.bfloat16).reshape(8, 16, 384)

    pl.semaphore_wait(barrier, CHUNKS * PER - 1)

    def post(r, carry):
        e, t = target_of(r, dp, tk)
        pltpu.make_async_remote_copy(
            src_ref=send.at[t * 8 + e], dst_ref=recv.at[r],
            send_sem=send_sem, recv_sem=recv_sem.at[r // PER],
            device_id=(e, t), device_id_type=MESH,
        ).start()
        return carry

    lax.fori_loop(1, CHUNKS * PER, post, 0)
    pltpu.make_async_copy(send.at[mine], recv.at[0], recv_sem.at[0]).start()
    load1.wait()
    load2.wait()
    which = lax.broadcasted_iota(jnp.int32, (PER * CAP, 8), 1) == dp

    def work(c, carry):
        span = pl.ds(c * PER, PER)
        pltpu.make_async_copy(recv.at[span], recv.at[span], recv_sem.at[c]).wait()
        got = recv[span].astype(jnp.float32)
        rows = jnp.concatenate([got[:, :CAP], got[:, CAP:]], axis=2)
        rows = rows.reshape(PER * CAP, 768).astype(jnp.bfloat16)
        total = jnp.zeros((PER * CAP, 768), jnp.float32)
        for j in range(4):
            hidden = jnp.dot(rows, w1[:, j * 768:(j + 1) * 768], preferred_element_type=jnp.float32)
            hidden = gelu(hidden).astype(jnp.bfloat16)
            total += jnp.dot(hidden, w2[j * 768:(j + 1) * 768, :], preferred_element_type=jnp.float32)
        logits = lax.dot_general(
            rows, router_ref[tk], (((1,), (1,)), ((), ())), preferred_element_type=jnp.float32
        )
        gate = jax.nn.sigmoid(jnp.sum(jnp.where(which, logits, 0.0), axis=1, keepdims=True))
        total = (total * gate).reshape(PER, CAP, 768)
        back_send[span] = jnp.concatenate(
            [total[:, :, :384], total[:, :, 384:]], axis=1
        ).astype(jnp.bfloat16)

        def reply(r, carry):
            e, t = source_of(r, dp, tk)
            pltpu.make_async_remote_copy(
                src_ref=back_send.at[r], dst_ref=back.at[mine],
                send_sem=back_send_sem, recv_sem=back_sem.at[c],
                device_id=(e, t), device_id_type=MESH,
            ).start()
            return carry

        lax.fori_loop(jnp.where(c == 0, 1, c * PER), (c + 1) * PER, reply, 0)

        @pl.when(c == 0)
        def _():
            pltpu.make_async_copy(back_send.at[0], back.at[mine], back_sem.at[0]).start()

        return carry

    lax.fori_loop(0, CHUNKS, work, 0)

    def finish(c, carry):
        span = pl.ds(c * PER, PER)
        pltpu.make_async_copy(back.at[span], back.at[span], back_sem.at[c]).wait()
        for q in range(4):
            t = ((tk // 4 + q) % 4) * 4 + (tk % 4 + c + 4 - q) % 4
            answers = back[pl.ds(t * 8, 8)].reshape(128, 384)
            moe = lax.dot_general(
                slots[t], answers, (((0,), (0,)), ((), ())), preferred_element_type=jnp.float32
            )
            moe = jnp.concatenate([moe[:16], moe[16:]], axis=1)
            out_ref[t] = layer_norm(normed[t].astype(jnp.float32) + moe).astype(jnp.bfloat16)
        return carry

    lax.fori_loop(0, CHUNKS, finish, 0)
    sent = pl.ds(1, CHUNKS * PER - 1)
    pltpu.make_async_copy(send.at[sent], send.at[sent], send_sem).wait()
    pltpu.make_async_copy(back_send.at[sent], back_send.at[sent], back_send_sem).wait()


def run_block(dense, cold, routes, router, w_in, w_out):
    vmem = pl.BlockSpec(memory_space=pltpu.VMEM)
    return pl.pallas_call(
        block_kernel,
        out_shape=jax.ShapeDtypeStruct((16, 16, 768), jnp.bfloat16),
        in_specs=[vmem] * 4 + [pl.BlockSpec(memory_space=pl.ANY)] * 2,
        out_specs=vmem,
        scratch_shapes=[
            pltpu.VMEM((768, 3072), jnp.bfloat16),
            pltpu.VMEM((3072, 768), jnp.bfloat16),
        ]
        + [pltpu.VMEM((128, 16, 384), jnp.bfloat16)] * 4
        + [
            pltpu.VMEM((16, 128, 32), jnp.bfloat16),
            pltpu.VMEM((16, 16, 768), jnp.bfloat16),
            pltpu.SemaphoreType.DMA((2,)),
            pltpu.SemaphoreType.DMA,
            pltpu.SemaphoreType.DMA((CHUNKS,)),
            pltpu.SemaphoreType.DMA,
            pltpu.SemaphoreType.DMA((CHUNKS,)),
        ],
        compiler_params=pltpu.CompilerParams(
            collective_id=0, has_side_effects=True, vmem_limit_bytes=48 * 1024 * 1024
        ),
        cost_estimate=pl.CostEstimate(
            flops=4 * 1024 * 768 * 3072, bytes_accessed=2 * 2 * 768 * 3072, transcendentals=0
        ),
    )(dense, cold, routes, router, w_in, w_out)


def shards(dense_tokens, cold_table, cold_ids, routes, router, w_in, w_out):
    samples = dense_tokens.shape[0]
    emb_width = cold_table.shape[1]
    rows_own = cold_table.shape[0]
    lists = cold_ids.shape[1]
    length = cold_ids.shape[2]
    gathered_ids = lax.all_gather(cold_ids, "dp", axis=0, tiled=True)
    base = lax.axis_index("dp") * rows_own
    factor = 1.0 / math.sqrt(length)
    local = gathered_ids - base
    inside = ((local >= 0) & (local < rows_own)).astype(jnp.bfloat16)
    found = jnp.take(cold_table, jnp.clip(local, 0, rows_own - 1), axis=0)
    summed = jnp.einsum("bgl,bgle->bge", inside, found, preferred_element_type=jnp.float32)
    cold = lax.psum_scatter(
        (summed.reshape(samples * lax.axis_size("dp"), lists * emb_width) * factor).astype(
            jnp.bfloat16
        ),
        "dp",
        scatter_dimension=0,
        tiled=True,
    )
    routes = routes.transpose(0, 2, 1)
    out = run_block(
        dense_tokens.transpose(1, 0, 2),
        cold,
        jnp.concatenate([routes, routes], axis=2),
        router.transpose(0, 2, 1),
        w_in[0, 0],
        w_out[0, 0],
    )
    return out.transpose(1, 0, 2)


def solution(mesh):
    return jax.shard_map(
        shards,
        mesh=mesh,
        in_specs=(
            P(("dp", "token"), None, None),
            P("dp", None),
            P(("dp", "token"), None, None),
            P(None, ("dp", "token"), None),
            P(),
            P("token", "dp", None, None),
            P("token", "dp", None, None),
        ),
        out_specs=P(("dp", "token"), None, None),
        check_vma=False,
    )
```

```python
import functools
import math

import jax
import jax.numpy as jnp
from jax import lax
from jax.experimental import pallas as pl
from jax.experimental.pallas import tpu as pltpu
from jax.sharding import PartitionSpec as P

CHUNKS = 4
PER = 32
CAP = 8
MESH = pl.DeviceIdType.MESH


def offsets(r):
    chunk, within = r // PER, r % PER
    dz, place = within // 8, within % 8
    return place // 2, place % 2, dz, (chunk + 4 - dz) % 4


def target_of(r, dp, tk):
    dx, dc, dz, dy = offsets(r)
    return (
        ((dp // 2 + dx) % 4) * 2 + (dp % 2 + dc) % 2,
        ((tk // 4 + dz) % 4) * 4 + (tk % 4 + dy) % 4,
    )


def source_of(r, dp, tk):
    dx, dc, dz, dy = offsets(r)
    return (
        ((dp // 2 + 4 - dx) % 4) * 2 + (dp % 2 + dc) % 2,
        ((tk // 4 + 4 - dz) % 4) * 4 + (tk % 4 + 4 - dy) % 4,
    )


def peer_of(k, dp, way):
    return ((dp // 2 + 4 + way * (k // 2)) % 4) * 2 + (dp % 2 + k) % 2


def layer_norm(value):
    mean = jnp.mean(value, axis=-1, keepdims=True)
    centred = value - mean
    var = jnp.mean(centred * centred, axis=-1, keepdims=True)
    return centred * lax.rsqrt(var + 1e-05)


def gelu(value):
    return 0.5 * value * (1.0 + lax.erf(value * math.sqrt(0.5)))


def block_kernel(
    dense_ref, ids_ref, routes_ref, router_ref, table_hbm, w1_hbm, w2_hbm, out_ref,
    w1, w2, send, recv, back_send, back, slots, normed,
    table, ids, counts, sums, part_send, part,
    w_sem, send_sem, recv_sem, back_send_sem, back_sem, id_send_sem, id_sem, part_send_sem, part_sem,
):
    dp, tk = lax.axis_index("dp"), lax.axis_index("token")
    mine = tk * 8 + dp
    load_table = pltpu.make_async_copy(table_hbm, table, w_sem.at[2])
    load_table.start()
    load1 = pltpu.make_async_copy(w1_hbm, w1, w_sem.at[0])
    load2 = pltpu.make_async_copy(w2_hbm, w2, w_sem.at[1])
    load1.start()
    load2.start()
    barrier = pltpu.get_barrier_semaphore()

    def greet(r, carry):
        pl.semaphore_signal(barrier, inc=1, device_id=target_of(r, dp, tk), device_id_type=MESH)
        return carry

    lax.fori_loop(1, CHUNKS * PER, greet, 0)

    expert = lax.broadcasted_iota(jnp.int32, (16, 8, 32), 1)
    picks = (routes_ref[:, 0:1, :] == expert) | (routes_ref[:, 1:2, :] == expert)
    row = lax.broadcasted_iota(jnp.int32, (32, 32), 0)
    col = lax.broadcasted_iota(jnp.int32, (32, 32), 1)
    before = jnp.where((row // 16 == col // 16) & (row < col), 1.0, 0.0).astype(jnp.bfloat16)
    ones = jnp.where(picks, 1.0, 0.0)
    place = jnp.dot(
        ones.reshape(128, 32).astype(jnp.bfloat16), before, preferred_element_type=jnp.float32
    ).reshape(16, 8, 32)
    place = jnp.where(picks, place, -1.0)
    slot = lax.broadcasted_iota(jnp.int32, (16, 16, 32), 1)
    half = lax.broadcasted_iota(jnp.int32, (16, 16, 32), 2) // 16
    number = jnp.where(slot // 8 == half, slot % 8, -2).astype(jnp.float32)
    for e in range(8):
        slots[:, e * 16:(e + 1) * 16, :] = jnp.where(
            place[:, e:e + 1, :] == number, 1.0, 0.0
        ).astype(jnp.bfloat16)

    pl.semaphore_wait(barrier, CHUNKS * PER - 1)
    for k in range(1, 8):
        pltpu.make_async_remote_copy(
            src_ref=ids_ref, dst_ref=ids.at[k], send_sem=id_send_sem.at[k - 1],
            recv_sem=id_sem.at[k - 1], device_id=(peer_of(k, dp, 1), tk), device_id_type=MESH,
        ).start()
    ids[0] = ids_ref[...]
    load_table.wait()
    own_rows = table.shape[0]
    diagonal = (
        lax.broadcasted_iota(jnp.int32, (16, 256), 0)
        == lax.broadcasted_iota(jnp.int32, (16, 256), 1) // 16
    )
    low_row = lax.broadcasted_iota(jnp.int32, (256, 256), 0).astype(jnp.float32).astype(jnp.bfloat16)
    one, none = jnp.ones((), jnp.bfloat16), jnp.zeros((), jnp.bfloat16)
    for part_no in range(2):
        for k in range(part_no * 4, part_no * 4 + 4):
            if k:
                pltpu.make_async_copy(ids.at[k], ids.at[k], id_sem.at[k - 1]).wait()

        def count(group, carry):
            local = ids[part_no * 4 + group // 6, pl.ds(group % 6, 1), :] - dp * own_rows
            inside = (local >= 0) & (local < own_rows)
            high = jnp.where(inside & diagonal, local // 256, -1)
            high = high.astype(jnp.float32).astype(jnp.bfloat16)
            low = jnp.where(inside, local % 256, 0).astype(jnp.float32).astype(jnp.bfloat16)
            lefts = jnp.concatenate(
                [jnp.where(high == float(i), one, none) for i in range(own_rows // 256)], axis=0
            )
            right = jnp.where(low_row == low, one, none)
            found = lax.dot_general(
                lefts, right, (((1,), (1,)), ((), ())), preferred_element_type=jnp.float32
            ).astype(jnp.bfloat16)
            rows = pl.ds(pl.multiple_of(group * 16, 16), 16)
            for i in range(own_rows // 256):
                counts[rows, i * 256:(i + 1) * 256] = found[i * 16:(i + 1) * 16]
            return carry

        lax.fori_loop(0, 24, count, 0)
        sums[...] = jnp.zeros_like(sums)

        def pool(step, carry):
            at = pl.ds(pl.multiple_of(step * 2048, 2048), 2048)
            sums[...] += jnp.dot(counts[:, at], table[at, :], preferred_element_type=jnp.float32)
            return carry

        lax.fori_loop(0, own_rows // 2048, pool, 0)
        pooled = (sums[...] * 0.25).astype(jnp.bfloat16).reshape(4, 96, 128)
        for k in range(part_no * 4, part_no * 4 + 4):
            if k == 0:
                part[0] = pooled[0]
            else:
                part_send[k] = pooled[k % 4]
                pltpu.make_async_remote_copy(
                    src_ref=part_send.at[k], dst_ref=part.at[k], send_sem=part_send_sem.at[k - 1],
                    recv_sem=part_sem.at[k - 1], device_id=(peer_of(k, dp, -1), tk),
                    device_id_type=MESH,
                ).start()
    for k in range(1, 8):
        pltpu.make_async_copy(part.at[k], part.at[k], part_sem.at[k - 1]).wait()
    cold = part[0].astype(jnp.float32)
    for k in range(1, 8):
        cold += part[k].astype(jnp.float32)
    cold = cold.astype(jnp.bfloat16)
    cold = jnp.concatenate([cold[g * 16:(g + 1) * 16] for g in range(6)], axis=1)

    features = [dense_ref[t] for t in range(15)] + [cold]
    for h in range(16):
        mixed = jnp.concatenate([f[:, h * 48:(h + 1) * 48] for f in features], axis=1)
        rows = layer_norm(mixed.astype(jnp.float32) + features[h].astype(jnp.float32))
        rows = rows.astype(jnp.bfloat16)
        normed[h] = rows
        halves = jnp.concatenate([rows[:, :384], rows[:, 384:]], axis=0)
        out = jnp.dot(slots[h], halves, preferred_element_type=jnp.float32)
        send[h * 8:(h + 1) * 8] = out.astype(jnp.bfloat16).reshape(8, 16, 384)

    def post(r, carry):
        e, t = target_of(r, dp, tk)
        pltpu.make_async_remote_copy(
            src_ref=send.at[t * 8 + e], dst_ref=recv.at[r],
            send_sem=send_sem, recv_sem=recv_sem.at[r // PER],
            device_id=(e, t), device_id_type=MESH,
        ).start()
        return carry

    lax.fori_loop(1, CHUNKS * PER, post, 0)
    pltpu.make_async_copy(send.at[mine], recv.at[0], recv_sem.at[0]).start()
    load1.wait()
    load2.wait()
    which = lax.broadcasted_iota(jnp.int32, (PER * CAP, 8), 1) == dp

    def work(c, carry):
        span = pl.ds(c * PER, PER)
        pltpu.make_async_copy(recv.at[span], recv.at[span], recv_sem.at[c]).wait()
        got = recv[span].astype(jnp.float32)
        rows = jnp.concatenate([got[:, :CAP], got[:, CAP:]], axis=2)
        rows = rows.reshape(PER * CAP, 768).astype(jnp.bfloat16)
        total = jnp.zeros((PER * CAP, 768), jnp.float32)
        for j in range(4):
            hidden = jnp.dot(rows, w1[:, j * 768:(j + 1) * 768], preferred_element_type=jnp.float32)
            hidden = gelu(hidden).astype(jnp.bfloat16)
            total += jnp.dot(hidden, w2[j * 768:(j + 1) * 768, :], preferred_element_type=jnp.float32)
        logits = lax.dot_general(
            rows, router_ref[tk], (((1,), (1,)), ((), ())), preferred_element_type=jnp.float32
        )
        gate = jax.nn.sigmoid(jnp.sum(jnp.where(which, logits, 0.0), axis=1, keepdims=True))
        total = (total * gate).reshape(PER, CAP, 768)
        back_send[span] = jnp.concatenate(
            [total[:, :, :384], total[:, :, 384:]], axis=1
        ).astype(jnp.bfloat16)

        def reply(r, carry):
            e, t = source_of(r, dp, tk)
            pltpu.make_async_remote_copy(
                src_ref=back_send.at[r], dst_ref=back.at[mine],
                send_sem=back_send_sem, recv_sem=back_sem.at[c],
                device_id=(e, t), device_id_type=MESH,
            ).start()
            return carry

        lax.fori_loop(jnp.where(c == 0, 1, c * PER), (c + 1) * PER, reply, 0)

        @pl.when(c == 0)
        def _():
            pltpu.make_async_copy(back_send.at[0], back.at[mine], back_sem.at[0]).start()

        return carry

    lax.fori_loop(0, CHUNKS, work, 0)

    def finish(c, carry):
        span = pl.ds(c * PER, PER)
        pltpu.make_async_copy(back.at[span], back.at[span], back_sem.at[c]).wait()
        for q in range(4):
            t = ((tk // 4 + q) % 4) * 4 + (tk % 4 + c + 4 - q) % 4
            answers = back[pl.ds(t * 8, 8)].reshape(128, 384)
            moe = lax.dot_general(
                slots[t], answers, (((0,), (0,)), ((), ())), preferred_element_type=jnp.float32
            )
            moe = jnp.concatenate([moe[:16], moe[16:]], axis=1)
            out_ref[t] = layer_norm(normed[t].astype(jnp.float32) + moe).astype(jnp.bfloat16)
        return carry

    lax.fori_loop(0, CHUNKS, finish, 0)
    for k in range(1, 8):
        pltpu.make_async_copy(ids_ref, ids_ref, id_send_sem.at[k - 1]).wait()
        pltpu.make_async_copy(part_send.at[k], part_send.at[k], part_send_sem.at[k - 1]).wait()
    sent = pl.ds(1, CHUNKS * PER - 1)
    pltpu.make_async_copy(send.at[sent], send.at[sent], send_sem).wait()
    pltpu.make_async_copy(back_send.at[sent], back_send.at[sent], back_send_sem).wait()


def run_block(dense, ids, routes, router, table, w_in, w_out):
    vmem = pl.BlockSpec(memory_space=pltpu.VMEM)
    return pl.pallas_call(
        block_kernel,
        out_shape=jax.ShapeDtypeStruct((16, 16, 768), jnp.bfloat16),
        in_specs=[vmem] * 4 + [pl.BlockSpec(memory_space=pl.ANY)] * 3,
        out_specs=vmem,
        scratch_shapes=[
            pltpu.VMEM((768, 3072), jnp.bfloat16),
            pltpu.VMEM((3072, 768), jnp.bfloat16),
        ]
        + [pltpu.VMEM((128, 16, 384), jnp.bfloat16)] * 4
        + [
            pltpu.VMEM((16, 128, 32), jnp.bfloat16),
            pltpu.VMEM((16, 16, 768), jnp.bfloat16),
            pltpu.VMEM(table.shape, jnp.bfloat16),
            pltpu.VMEM((8, 8, 256), jnp.int32),
            pltpu.VMEM((384, table.shape[0]), jnp.bfloat16),
            pltpu.VMEM((384, 128), jnp.float32),
            pltpu.VMEM((8, 96, 128), jnp.bfloat16),
            pltpu.VMEM((8, 96, 128), jnp.bfloat16),
            pltpu.SemaphoreType.DMA((3,)),
            pltpu.SemaphoreType.DMA,
            pltpu.SemaphoreType.DMA((CHUNKS,)),
            pltpu.SemaphoreType.DMA,
            pltpu.SemaphoreType.DMA((CHUNKS,)),
        ]
        + [pltpu.SemaphoreType.DMA((7,))] * 4,
        compiler_params=pltpu.CompilerParams(
            collective_id=0, has_side_effects=True, vmem_limit_bytes=58 * 1024 * 1024
        ),
        cost_estimate=pl.CostEstimate(
            flops=4 * 1024 * 768 * 3072, bytes_accessed=2 * 2 * 768 * 3072, transcendentals=0
        ),
    )(dense, ids, routes, router, table, w_in, w_out)


def shards(dense_tokens, cold_table, cold_ids, routes, router, w_in, w_out):
    ids = cold_ids.transpose(1, 0, 2).reshape(6, 256)
    ids = jnp.concatenate([ids, ids[:2]], axis=0)
    routes = routes.transpose(0, 2, 1)
    out = run_block(
        dense_tokens.transpose(1, 0, 2),
        ids,
        jnp.concatenate([routes, routes], axis=2),
        router.transpose(0, 2, 1),
        cold_table,
        w_in[0, 0],
        w_out[0, 0],
    )
    return out.transpose(1, 0, 2)


def solution(mesh):
    return jax.shard_map(
        shards,
        mesh=mesh,
        in_specs=(
            P(("dp", "token"), None, None),
            P("dp", None),
            P(("dp", "token"), None, None),
            P(None, ("dp", "token"), None),
            P(),
            P("token", "dp", None, None),
            P("token", "dp", None, None),
        ),
        out_specs=P(("dp", "token"), None, None),
        check_vma=False,
    )
```

```python
import functools
import math

import jax
import jax.numpy as jnp
from jax import lax
from jax.experimental import pallas as pl
from jax.experimental.pallas import tpu as pltpu
from jax.sharding import PartitionSpec as P

CHUNKS = 4
PER = 32
CAP = 8
MESH = pl.DeviceIdType.MESH


def peer_of(k, dp, way):
    return ((dp // 2 + 4 + way * (k // 2)) % 4) * 2 + (dp % 2 + k) % 2


def layer_norm(value):
    mean = jnp.mean(value, axis=-1, keepdims=True)
    centred = value - mean
    var = jnp.mean(centred * centred, axis=-1, keepdims=True)
    return centred * lax.rsqrt(var + 1e-05)


def gelu(value):
    return 0.5 * value * (1.0 + lax.erf(value * math.sqrt(0.5)))


def block_kernel(
    dense_ref, ids_ref, routes_ref, router_ref, table_hbm, w1_hbm, w2_hbm, out_ref,
    w1, w2, send, recv, back_send, back, slots, normed,
    table, own_ids, ids, counts, sums, part_send, part,
    w_sem, send_sem, recv_sem, back_send_sem, back_sem, id_send_sem, id_sem, part_send_sem, part_sem,
):
    dp, tk = lax.axis_index("dp"), lax.axis_index("token")
    mine = tk * 8 + dp
    load_table = pltpu.make_async_copy(table_hbm, table, w_sem.at[2])
    load_table.start()
    load1 = pltpu.make_async_copy(w1_hbm, w1, w_sem.at[0])
    load2 = pltpu.make_async_copy(w2_hbm, w2, w_sem.at[1])
    load1.start()
    load2.start()
    diagonal = (
        lax.broadcasted_iota(jnp.int32, (16, 256), 0)
        == lax.broadcasted_iota(jnp.int32, (16, 256), 1) // 16
    )
    barrier = pltpu.get_barrier_semaphore()

    x, core, z, y = dp // 2, dp % 2, tk // 4, tk % 4
    zs, ys = [(z + i) % 4 for i in range(4)], [(y + i) % 4 for i in range(4)]
    experts = [((x + p // 2) % 4) * 2 + (core + p) % 2 for p in range(8)]
    givers = [experts[(8 - p // 2 * 2) % 8 + p % 2] for p in range(8)]

    def tokens(chunk, way):
        return [
            zs[way * q % 4] * 4 + (y + 4 + way * (chunk + 4 - q)) % 4
            if not isinstance(chunk, int) else zs[way * q % 4] * 4 + ys[way * (chunk - q) % 4]
            for q in range(4)
        ]

    for chunk in range(CHUNKS):
        for q, t in enumerate(tokens(chunk, 1)):
            for p, e in enumerate(experts):
                if chunk + q + p:
                    pl.semaphore_signal(barrier, inc=1, device_id=(e, t), device_id_type=MESH)

    for g in range(6):
        wide = jnp.concatenate([ids_ref[g]] * 16, axis=1)
        own_ids[g:g + 1, :] = jnp.sum(jnp.where(diagonal, wide, 0), axis=0, keepdims=True)
    own_ids[6:8, :] = jnp.zeros((2, 256), jnp.int32)
    own_routes = jnp.concatenate([routes_ref[...]] * 2, axis=2)
    expert = lax.broadcasted_iota(jnp.int32, (16, 8, 32), 1)
    picks = (own_routes[:, 0:1, :] == expert) | (own_routes[:, 1:2, :] == expert)
    row = lax.broadcasted_iota(jnp.int32, (32, 32), 0)
    col = lax.broadcasted_iota(jnp.int32, (32, 32), 1)
    before = jnp.where((row // 16 == col // 16) & (row < col), 1.0, 0.0).astype(jnp.bfloat16)
    ones = jnp.where(picks, 1.0, 0.0)
    place = jnp.dot(
        ones.reshape(128, 32).astype(jnp.bfloat16), before, preferred_element_type=jnp.float32
    ).reshape(16, 8, 32)
    place = jnp.where(picks, place, -1.0)
    slot = lax.broadcasted_iota(jnp.int32, (16, 16, 32), 1)
    half = lax.broadcasted_iota(jnp.int32, (16, 16, 32), 2) // 16
    number = jnp.where(slot // 8 == half, slot % 8, -2).astype(jnp.float32)
    for e in range(8):
        slots[:, e * 16:(e + 1) * 16, :] = jnp.where(
            place[:, e:e + 1, :] == number, 1.0, 0.0
        ).astype(jnp.bfloat16)

    pl.semaphore_wait(barrier, CHUNKS * PER - 1)
    for k in range(1, 8):
        pltpu.make_async_remote_copy(
            src_ref=own_ids, dst_ref=ids.at[k], send_sem=id_send_sem.at[k - 1],
            recv_sem=id_sem.at[k - 1], device_id=(peer_of(k, dp, 1), tk), device_id_type=MESH,
        ).start()
    ids[0] = own_ids[...]
    load_table.wait()
    own_rows = table.shape[0]
    low_row = lax.broadcasted_iota(jnp.int32, (256, 256), 0).astype(jnp.float32).astype(jnp.bfloat16)
    one, none = jnp.ones((), jnp.bfloat16), jnp.zeros((), jnp.bfloat16)
    for part_no in range(2):
        for k in range(part_no * 4, part_no * 4 + 4):
            if k:
                pltpu.make_async_copy(ids.at[k], ids.at[k], id_sem.at[k - 1]).wait()

        def count(step, carry):
            for u in range(6):
                group = step * 6 + u
                local = ids[part_no * 4 + group // 6, pl.ds(group % 6, 1), :] - dp * own_rows
                inside = (local >= 0) & (local < own_rows)
                high = jnp.where(inside & diagonal, local // 256, -1)
                high = high.astype(jnp.float32).astype(jnp.bfloat16)
                low = jnp.where(inside, local % 256, 0).astype(jnp.float32).astype(jnp.bfloat16)
                right = jnp.where(low_row == low, one, none)
                rows = pl.ds(pl.multiple_of(group * 16, 16), 16)
                for v in range(4):
                    lefts = jnp.concatenate(
                        [jnp.where(high == float(v * 16 + i), one, none) for i in range(16)], axis=0
                    )
                    found = lax.dot_general(
                        lefts, right, (((1,), (1,)), ((), ())), preferred_element_type=jnp.float32
                    ).astype(jnp.bfloat16)
                    for i in range(16):
                        at = (v * 16 + i) * 256
                        counts[rows, at:at + 256] = found[i * 16:(i + 1) * 16]
            return carry

        lax.fori_loop(0, 24 // 6, count, 0)
        sums[...] = jnp.zeros_like(sums)

        def pool(step, carry):
            at = pl.ds(pl.multiple_of(step * 8192, 8192), 8192)
            sums[...] += jnp.dot(counts[:, at], table[at, :], preferred_element_type=jnp.float32)
            return carry

        lax.fori_loop(0, own_rows // 8192, pool, 0)
        pooled = (sums[...] * 0.25).astype(jnp.bfloat16).reshape(4, 96, 128)
        for k in range(part_no * 4, part_no * 4 + 4):
            if k == 0:
                part[0] = pooled[0]
            else:
                part_send[k] = pooled[k % 4]
                pltpu.make_async_remote_copy(
                    src_ref=part_send.at[k], dst_ref=part.at[k], send_sem=part_send_sem.at[k - 1],
                    recv_sem=part_sem.at[k - 1], device_id=(peer_of(k, dp, -1), tk),
                    device_id_type=MESH,
                ).start()
    for k in range(1, 8):
        pltpu.make_async_copy(part.at[k], part.at[k], part_sem.at[k - 1]).wait()
    cold = part[0].astype(jnp.float32)
    for k in range(1, 8):
        cold += part[k].astype(jnp.float32)
    cold = cold.astype(jnp.bfloat16)
    cold = jnp.concatenate([cold[g * 16:(g + 1) * 16] for g in range(6)], axis=1)

    features = [dense_ref[t] for t in range(15)] + [cold]
    for h in range(16):
        mixed = jnp.concatenate([f[:, h * 48:(h + 1) * 48] for f in features], axis=1)
        rows = layer_norm(mixed.astype(jnp.float32) + features[h].astype(jnp.float32))
        rows = rows.astype(jnp.bfloat16)
        normed[h] = rows
        halves = jnp.concatenate([rows[:, :384], rows[:, 384:]], axis=0)
        out = jnp.dot(slots[h], halves, preferred_element_type=jnp.float32)
        send[h * 8:(h + 1) * 8] = out.astype(jnp.bfloat16).reshape(8, 16, 384)

    for chunk in range(CHUNKS):
        for q, t in enumerate(tokens(chunk, 1)):
            for p, e in enumerate(experts):
                r = chunk * PER + q * 8 + p
                if r:
                    pltpu.make_async_remote_copy(
                        src_ref=send.at[t * 8 + e], dst_ref=recv.at[r],
                        send_sem=send_sem, recv_sem=recv_sem.at[chunk],
                        device_id=(e, t), device_id_type=MESH,
                    ).start()
    pltpu.make_async_copy(send.at[mine], recv.at[0], recv_sem.at[0]).start()
    load1.wait()
    load2.wait()
    which = lax.broadcasted_iota(jnp.int32, (PER * CAP, 8), 1) == dp

    def work(c, carry):
        span = pl.ds(c * PER, PER)
        pltpu.make_async_copy(recv.at[span], recv.at[span], recv_sem.at[c]).wait()
        got = recv[span].astype(jnp.float32)
        rows = jnp.concatenate([got[:, :CAP], got[:, CAP:]], axis=2)
        rows = rows.reshape(PER * CAP, 768).astype(jnp.bfloat16)
        total = jnp.zeros((PER * CAP, 768), jnp.float32)
        for j in range(4):
            hidden = jnp.dot(rows, w1[:, j * 768:(j + 1) * 768], preferred_element_type=jnp.float32)
            hidden = gelu(hidden).astype(jnp.bfloat16)
            total += jnp.dot(hidden, w2[j * 768:(j + 1) * 768, :], preferred_element_type=jnp.float32)
        logits = lax.dot_general(
            rows, router_ref[tk], (((1,), (1,)), ((), ())), preferred_element_type=jnp.float32
        )
        gate = jax.nn.sigmoid(jnp.sum(jnp.where(which, logits, 0.0), axis=1, keepdims=True))
        total = (total * gate).reshape(PER, CAP, 768)
        back_send[span] = jnp.concatenate(
            [total[:, :, :384], total[:, :, 384:]], axis=1
        ).astype(jnp.bfloat16)

        for q, t in enumerate(tokens(c, -1)):
            for p, e in enumerate(givers):
                r = c * PER + q * 8 + p
                away = pltpu.make_async_remote_copy(
                    src_ref=back_send.at[r], dst_ref=back.at[mine],
                    send_sem=back_send_sem, recv_sem=back_sem.at[c],
                    device_id=(e, t), device_id_type=MESH,
                )
                if q + p:
                    away.start()
                else:
                    pl.when(c > 0)(away.start)

        @pl.when(c == 0)
        def _():
            pltpu.make_async_copy(back_send.at[0], back.at[mine], back_sem.at[0]).start()

        return carry

    lax.fori_loop(0, CHUNKS, work, 0)

    def finish(c, carry):
        span = pl.ds(c * PER, PER)
        pltpu.make_async_copy(back.at[span], back.at[span], back_sem.at[c]).wait()
        for t in tokens(c, 1):
            answers = back[pl.ds(t * 8, 8)].reshape(128, 384)
            moe = lax.dot_general(
                slots[t], answers, (((0,), (0,)), ((), ())), preferred_element_type=jnp.float32
            )
            moe = jnp.concatenate([moe[:16], moe[16:]], axis=1)
            out_ref[t] = layer_norm(normed[t].astype(jnp.float32) + moe).astype(jnp.bfloat16)
        return carry

    lax.fori_loop(0, CHUNKS, finish, 0)
    for k in range(1, 8):
        pltpu.make_async_copy(own_ids, own_ids, id_send_sem.at[k - 1]).wait()
        pltpu.make_async_copy(part_send.at[k], part_send.at[k], part_send_sem.at[k - 1]).wait()
    sent = pl.ds(1, CHUNKS * PER - 1)
    pltpu.make_async_copy(send.at[sent], send.at[sent], send_sem).wait()
    pltpu.make_async_copy(back_send.at[sent], back_send.at[sent], back_send_sem).wait()


def run_block(dense, ids, routes, router, table, w_in, w_out):
    vmem = pl.BlockSpec(memory_space=pltpu.VMEM)
    return pl.pallas_call(
        block_kernel,
        out_shape=jax.ShapeDtypeStruct((16, 16, 768), jnp.bfloat16),
        in_specs=[vmem] * 4 + [pl.BlockSpec(memory_space=pl.ANY)] * 3,
        out_specs=vmem,
        scratch_shapes=[
            pltpu.VMEM((768, 3072), jnp.bfloat16),
            pltpu.VMEM((3072, 768), jnp.bfloat16),
        ]
        + [pltpu.VMEM((128, 16, 384), jnp.bfloat16)] * 4
        + [
            pltpu.VMEM((16, 128, 32), jnp.bfloat16),
            pltpu.VMEM((16, 16, 768), jnp.bfloat16),
            pltpu.VMEM(table.shape, jnp.bfloat16),
            pltpu.VMEM((8, 256), jnp.int32),
            pltpu.VMEM((8, 8, 256), jnp.int32),
            pltpu.VMEM((384, table.shape[0]), jnp.bfloat16),
            pltpu.VMEM((384, 128), jnp.float32),
            pltpu.VMEM((8, 96, 128), jnp.bfloat16),
            pltpu.VMEM((8, 96, 128), jnp.bfloat16),
            pltpu.SemaphoreType.DMA((3,)),
            pltpu.SemaphoreType.DMA,
            pltpu.SemaphoreType.DMA((CHUNKS,)),
            pltpu.SemaphoreType.DMA,
            pltpu.SemaphoreType.DMA((CHUNKS,)),
        ]
        + [pltpu.SemaphoreType.DMA((7,))] * 4,
        compiler_params=pltpu.CompilerParams(
            collective_id=0, has_side_effects=True, vmem_limit_bytes=58 * 1024 * 1024
        ),
        cost_estimate=pl.CostEstimate(
            flops=4 * 1024 * 768 * 3072, bytes_accessed=2 * 2 * 768 * 3072, transcendentals=0
        ),
    )(dense, ids, routes, router, table, w_in, w_out)


def shards(dense_tokens, cold_table, cold_ids, routes, router, w_in, w_out):
    out = run_block(
        dense_tokens.transpose(1, 0, 2),
        cold_ids.transpose(1, 0, 2),
        routes.transpose(0, 2, 1),
        router.transpose(0, 2, 1),
        cold_table,
        w_in[0, 0],
        w_out[0, 0],
    )
    return out.transpose(1, 0, 2)


def solution(mesh):
    return jax.shard_map(
        shards,
        mesh=mesh,
        in_specs=(
            P(("dp", "token"), None, None),
            P("dp", None),
            P(("dp", "token"), None, None),
            P(None, ("dp", "token"), None),
            P(),
            P("token", "dp", None, None),
            P("token", "dp", None, None),
        ),
        out_specs=P(("dp", "token"), None, None),
        check_vma=False,
    )
```

```python
import functools
import math

import jax
import jax.numpy as jnp
from jax import lax
from jax.experimental import pallas as pl
from jax.experimental.pallas import tpu as pltpu
from jax.sharding import PartitionSpec as P

CHUNKS = 4
PER = 32
CAP = 8
MESH = pl.DeviceIdType.MESH


def peer_of(k, dp, way):
    return ((dp // 2 + 4 + way * (k // 2)) % 4) * 2 + (dp % 2 + k) % 2


def layer_norm(value):
    mean = jnp.mean(value, axis=-1, keepdims=True)
    centred = value - mean
    var = jnp.mean(centred * centred, axis=-1, keepdims=True)
    return centred * lax.rsqrt(var + 1e-05)


def gelu(value):
    return 0.5 * value * (1.0 + lax.erf(value * math.sqrt(0.5)))


def block_kernel(
    dense_ref, ids_ref, routes_ref, router_ref, table_hbm, w1_hbm, w2_hbm, out_ref,
    w1, w2, send, recv, back_send, back, slots, normed,
    table, own_ids, ids, counts, sums, part_send, part,
    w_sem, send_sem, recv_sem, back_send_sem, back_sem, id_send_sem, id_sem, part_send_sem, part_sem,
):
    dp, tk = lax.axis_index("dp"), lax.axis_index("token")
    mine = tk * 8 + dp
    load_table = pltpu.make_async_copy(table_hbm, table, w_sem.at[2])
    load_table.start()
    load1 = pltpu.make_async_copy(w1_hbm, w1, w_sem.at[0])
    load2 = pltpu.make_async_copy(w2_hbm, w2, w_sem.at[1])
    load1.start()
    load2.start()
    diagonal = (
        lax.broadcasted_iota(jnp.int32, (16, 256), 0)
        == lax.broadcasted_iota(jnp.int32, (16, 256), 1) // 16
    )
    barrier = pltpu.get_barrier_semaphore()

    x, core, z, y = dp // 2, dp % 2, tk // 4, tk % 4
    zs, ys = [(z + i) % 4 for i in range(4)], [(y + i) % 4 for i in range(4)]
    experts = [((x + p // 2) % 4) * 2 + (core + p) % 2 for p in range(8)]
    givers = [experts[(8 - p // 2 * 2) % 8 + p % 2] for p in range(8)]

    def tokens(chunk, way):
        return [
            zs[way * q % 4] * 4 + (y + 4 + way * (chunk + 4 - q)) % 4
            if not isinstance(chunk, int) else zs[way * q % 4] * 4 + ys[way * (chunk - q) % 4]
            for q in range(4)
        ]

    for chunk in range(CHUNKS):
        for q, t in enumerate(tokens(chunk, 1)):
            for p, e in enumerate(experts):
                if chunk + q + p:
                    pl.semaphore_signal(barrier, inc=1, device_id=(e, t), device_id_type=MESH)

    for g in range(6):
        wide = jnp.concatenate([ids_ref[g]] * 16, axis=1)
        own_ids[g:g + 1, :] = jnp.sum(jnp.where(diagonal, wide, 0), axis=0, keepdims=True)
    own_ids[6:8, :] = jnp.zeros((2, 256), jnp.int32)
    ids[0] = own_ids[...]
    own_rows = table.shape[0]
    low_row = lax.broadcasted_iota(jnp.int32, (256, 256), 0).astype(jnp.float32).astype(jnp.bfloat16)
    one, none = jnp.ones((), jnp.bfloat16), jnp.zeros((), jnp.bfloat16)

    def count(k):
        for g in range(6):
            local = ids[k, g:g + 1, :] - dp * own_rows
            inside = (local >= 0) & (local < own_rows)
            high = jnp.where(inside & diagonal, local // 256, -1)
            high = high.astype(jnp.float32).astype(jnp.bfloat16)
            low = jnp.where(inside, local % 256, 0).astype(jnp.float32).astype(jnp.bfloat16)
            right = jnp.where(low_row == low, one, none).astype(jnp.float8_e4m3fn)
            row = (k % 4) * 96 + g * 16
            for v in range(own_rows // 4096):
                lefts = jnp.concatenate(
                    [jnp.where(high == float(v * 16 + i), one, none) for i in range(16)], axis=0
                ).astype(jnp.float8_e4m3fn)
                found = lax.dot_general(
                    lefts, right, (((1,), (1,)), ((), ())), preferred_element_type=jnp.float32
                ).astype(jnp.bfloat16)
                for i in range(16):
                    at = (v * 16 + i) * 256
                    counts[row:row + 16, at:at + 256] = found[i * 16:(i + 1) * 16]

    count(0)
    pl.semaphore_wait(barrier, CHUNKS * PER - 1)
    for k in range(1, 8):
        pltpu.make_async_remote_copy(
            src_ref=own_ids, dst_ref=ids.at[k], send_sem=id_send_sem.at[k - 1],
            recv_sem=id_sem.at[k - 1], device_id=(peer_of(k, dp, 1), tk), device_id_type=MESH,
        ).start()
    own_routes = jnp.concatenate([routes_ref[...]] * 2, axis=2)
    expert = lax.broadcasted_iota(jnp.int32, (16, 8, 32), 1)
    picks = (own_routes[:, 0:1, :] == expert) | (own_routes[:, 1:2, :] == expert)
    row = lax.broadcasted_iota(jnp.int32, (32, 32), 0)
    col = lax.broadcasted_iota(jnp.int32, (32, 32), 1)
    before = jnp.where((row // 16 == col // 16) & (row < col), 1.0, 0.0).astype(jnp.bfloat16)
    ones = jnp.where(picks, 1.0, 0.0)
    place = jnp.dot(
        ones.reshape(128, 32).astype(jnp.bfloat16), before, preferred_element_type=jnp.float32
    ).reshape(16, 8, 32)
    place = jnp.where(picks, place, -1.0)
    slot = lax.broadcasted_iota(jnp.int32, (16, 16, 32), 1)
    half = lax.broadcasted_iota(jnp.int32, (16, 16, 32), 2) // 16
    number = jnp.where(slot // 8 == half, slot % 8, -2).astype(jnp.float32)
    for e in range(8):
        slots[:, e * 16:(e + 1) * 16, :] = jnp.where(
            place[:, e:e + 1, :] == number, 1.0, 0.0
        ).astype(jnp.bfloat16)

    for part_no in range(2):
        for k in range(part_no * 4, part_no * 4 + 4):
            if k:
                pltpu.make_async_copy(ids.at[k], ids.at[k], id_sem.at[k - 1]).wait()
                count(k)
        sums[...] = jnp.zeros_like(sums)
        if part_no == 0:
            load_table.wait()

        def pool(step, carry):
            at = pl.ds(pl.multiple_of(step * 8192, 8192), 8192)
            sums[...] += jnp.dot(counts[:, at], table[at, :], preferred_element_type=jnp.float32)
            return carry

        lax.fori_loop(0, own_rows // 8192, pool, 0)
        pooled = (sums[...] * 0.25).astype(jnp.bfloat16).reshape(4, 96, 128)
        for k in range(part_no * 4, part_no * 4 + 4):
            if k == 0:
                part[0] = pooled[0]
            else:
                part_send[k] = pooled[k % 4]
                pltpu.make_async_remote_copy(
                    src_ref=part_send.at[k], dst_ref=part.at[k], send_sem=part_send_sem.at[k - 1],
                    recv_sem=part_sem.at[k - 1], device_id=(peer_of(k, dp, -1), tk),
                    device_id_type=MESH,
                ).start()
    for k in range(1, 8):
        pltpu.make_async_copy(part.at[k], part.at[k], part_sem.at[k - 1]).wait()
    cold = part[0].astype(jnp.float32)
    for k in range(1, 8):
        cold += part[k].astype(jnp.float32)
    cold = cold.astype(jnp.bfloat16)
    cold = jnp.concatenate([cold[g * 16:(g + 1) * 16] for g in range(6)], axis=1)

    features = [dense_ref[t] for t in range(15)] + [cold]
    for h in range(16):
        mixed = jnp.concatenate([f[:, h * 48:(h + 1) * 48] for f in features], axis=1)
        rows = layer_norm(mixed.astype(jnp.float32) + features[h].astype(jnp.float32))
        rows = rows.astype(jnp.bfloat16)
        normed[h] = rows
    for chunk in range(CHUNKS):
        for q, t in enumerate(tokens(chunk, 1)):
            rows = normed[t]
            halves = jnp.concatenate([rows[:, :384], rows[:, 384:]], axis=0)
            out = jnp.dot(slots[t], halves, preferred_element_type=jnp.float32)
            send[pl.ds(t * 8, 8)] = out.astype(jnp.bfloat16).reshape(8, 16, 384)
            for p, e in enumerate(experts):
                r = chunk * PER + q * 8 + p
                if r:
                    pltpu.make_async_remote_copy(
                        src_ref=send.at[t * 8 + e], dst_ref=recv.at[r],
                        send_sem=send_sem, recv_sem=recv_sem.at[chunk],
                        device_id=(e, t), device_id_type=MESH,
                    ).start()
    pltpu.make_async_copy(send.at[mine], recv.at[0], recv_sem.at[0]).start()
    load1.wait()
    load2.wait()
    which = lax.broadcasted_iota(jnp.int32, (PER * CAP, 8), 1) == dp

    def work(c, carry):
        span = pl.ds(c * PER, PER)
        pltpu.make_async_copy(recv.at[span], recv.at[span], recv_sem.at[c]).wait()
        got = recv[span].astype(jnp.float32)
        rows = jnp.concatenate([got[:, :CAP], got[:, CAP:]], axis=2)
        rows = rows.reshape(PER * CAP, 768).astype(jnp.bfloat16)
        total = jnp.zeros((PER * CAP, 768), jnp.float32)
        for j in range(4):
            hidden = jnp.dot(rows, w1[:, j * 768:(j + 1) * 768], preferred_element_type=jnp.float32)
            hidden = gelu(hidden).astype(jnp.bfloat16)
            total += jnp.dot(hidden, w2[j * 768:(j + 1) * 768, :], preferred_element_type=jnp.float32)
        logits = lax.dot_general(
            rows, router_ref[tk], (((1,), (1,)), ((), ())), preferred_element_type=jnp.float32
        )
        gate = jax.nn.sigmoid(jnp.sum(jnp.where(which, logits, 0.0), axis=1, keepdims=True))
        total = (total * gate).reshape(PER, CAP, 768)
        back_send[span] = jnp.concatenate(
            [total[:, :, :384], total[:, :, 384:]], axis=1
        ).astype(jnp.bfloat16)

        for q, t in enumerate(tokens(c, -1)):
            for p, e in enumerate(givers):
                r = c * PER + q * 8 + p
                away = pltpu.make_async_remote_copy(
                    src_ref=back_send.at[r], dst_ref=back.at[mine],
                    send_sem=back_send_sem, recv_sem=back_sem.at[c],
                    device_id=(e, t), device_id_type=MESH,
                )
                if q + p:
                    away.start()
                else:
                    pl.when(c > 0)(away.start)

        @pl.when(c == 0)
        def _():
            pltpu.make_async_copy(back_send.at[0], back.at[mine], back_sem.at[0]).start()

        return carry

    lax.fori_loop(0, CHUNKS, work, 0)

    def finish(c, carry):
        span = pl.ds(c * PER, PER)
        pltpu.make_async_copy(back.at[span], back.at[span], back_sem.at[c]).wait()
        for t in tokens(c, 1):
            answers = back[pl.ds(t * 8, 8)].reshape(128, 384)
            moe = lax.dot_general(
                slots[t], answers, (((0,), (0,)), ((), ())), preferred_element_type=jnp.float32
            )
            moe = jnp.concatenate([moe[:16], moe[16:]], axis=1)
            out_ref[t] = layer_norm(normed[t].astype(jnp.float32) + moe).astype(jnp.bfloat16)
        return carry

    lax.fori_loop(0, CHUNKS, finish, 0)
    for k in range(1, 8):
        pltpu.make_async_copy(own_ids, own_ids, id_send_sem.at[k - 1]).wait()
        pltpu.make_async_copy(part_send.at[k], part_send.at[k], part_send_sem.at[k - 1]).wait()
    sent = pl.ds(1, CHUNKS * PER - 1)
    pltpu.make_async_copy(send.at[sent], send.at[sent], send_sem).wait()
    pltpu.make_async_copy(back_send.at[sent], back_send.at[sent], back_send_sem).wait()


def run_block(dense, ids, routes, router, table, w_in, w_out):
    vmem = pl.BlockSpec(memory_space=pltpu.VMEM)
    return pl.pallas_call(
        block_kernel,
        out_shape=jax.ShapeDtypeStruct((16, 16, 768), jnp.bfloat16),
        in_specs=[vmem] * 4 + [pl.BlockSpec(memory_space=pl.ANY)] * 3,
        out_specs=vmem,
        scratch_shapes=[
            pltpu.VMEM((768, 3072), jnp.bfloat16),
            pltpu.VMEM((3072, 768), jnp.bfloat16),
        ]
        + [pltpu.VMEM((128, 16, 384), jnp.bfloat16)] * 4
        + [
            pltpu.VMEM((16, 128, 32), jnp.bfloat16),
            pltpu.VMEM((16, 16, 768), jnp.bfloat16),
            pltpu.VMEM(table.shape, jnp.bfloat16),
            pltpu.VMEM((8, 256), jnp.int32),
            pltpu.VMEM((8, 8, 256), jnp.int32),
            pltpu.VMEM((384, table.shape[0]), jnp.bfloat16),
            pltpu.VMEM((384, 128), jnp.float32),
            pltpu.VMEM((8, 96, 128), jnp.bfloat16),
            pltpu.VMEM((8, 96, 128), jnp.bfloat16),
            pltpu.SemaphoreType.DMA((3,)),
            pltpu.SemaphoreType.DMA,
            pltpu.SemaphoreType.DMA((CHUNKS,)),
            pltpu.SemaphoreType.DMA,
            pltpu.SemaphoreType.DMA((CHUNKS,)),
        ]
        + [pltpu.SemaphoreType.DMA((7,))] * 4,
        compiler_params=pltpu.CompilerParams(
            collective_id=0, has_side_effects=True, vmem_limit_bytes=58 * 1024 * 1024
        ),
        cost_estimate=pl.CostEstimate(
            flops=4 * 1024 * 768 * 3072, bytes_accessed=2 * 2 * 768 * 3072, transcendentals=0
        ),
    )(dense, ids, routes, router, table, w_in, w_out)


def shards(dense_tokens, cold_table, cold_ids, routes, router, w_in, w_out):
    out = run_block(
        dense_tokens.transpose(1, 0, 2),
        cold_ids.transpose(1, 0, 2),
        routes.transpose(0, 2, 1),
        router.transpose(0, 2, 1),
        cold_table,
        w_in[0, 0],
        w_out[0, 0],
    )
    return out.transpose(1, 0, 2)


def solution(mesh):
    return jax.shard_map(
        shards,
        mesh=mesh,
        in_specs=(
            P(("dp", "token"), None, None),
            P("dp", None),
            P(("dp", "token"), None, None),
            P(None, ("dp", "token"), None),
            P(),
            P("token", "dp", None, None),
            P("token", "dp", None, None),
        ),
        out_specs=P(("dp", "token"), None, None),
        check_vma=False,
    )
```

```python
import functools
import math

import jax
import jax.numpy as jnp
from jax import lax
from jax.experimental import pallas as pl
from jax.experimental.pallas import tpu as pltpu
from jax.sharding import PartitionSpec as P

CHUNKS = 4
PER = 32
CAP = 8
F8 = jnp.float8_e4m3fn
MESH = pl.DeviceIdType.MESH


def peer_of(k, dp, way):
    return ((dp // 2 + 4 + way * (k // 2)) % 4) * 2 + (dp % 2 + k) % 2


def layer_norm(value):
    mean = jnp.mean(value, axis=-1, keepdims=True)
    centred = value - mean
    var = jnp.mean(centred * centred, axis=-1, keepdims=True)
    return centred * lax.rsqrt(var + 1e-05)


def gelu(value):
    return 0.5 * value * (1.0 + lax.erf(value * math.sqrt(0.5)))


def block_kernel(
    dense_hbm, ids_hbm, routes_hbm, router_hbm, table_hbm, w1_hbm, w2_hbm, out_ref,
    dense_ref, ids_ref, routes_ref, router_ref, w1, w2, send, recv, back_send, back, slots, normed,
    table, pair, own_ids, ids, counts, sums, part_send, part,
    w_sem, send_sem, recv_sem, back_send_sem, back_sem, id_send_sem, id_sem, part_send_sem, part_sem,
):
    dp, tk = lax.axis_index("dp"), lax.axis_index("token")
    mine = tk * 8 + dp
    load_ids = pltpu.make_async_copy(ids_hbm, ids_ref, w_sem.at[3])
    load_routes = pltpu.make_async_copy(routes_hbm, routes_ref, w_sem.at[4])
    load_dense = pltpu.make_async_copy(dense_hbm, dense_ref, w_sem.at[5])
    load_router = pltpu.make_async_copy(router_hbm, router_ref, w_sem.at[6])
    load_ids.start()
    load_routes.start()
    load_dense.start()
    load_router.start()
    load_table = pltpu.make_async_copy(table_hbm, table, w_sem.at[2])
    load_table.start()
    load1 = pltpu.make_async_copy(w1_hbm, w1, w_sem.at[0])
    load2 = pltpu.make_async_copy(w2_hbm, w2, w_sem.at[1])
    load1.start()
    load2.start()
    diagonal = (
        lax.broadcasted_iota(jnp.int32, (16, 256), 0)
        == lax.broadcasted_iota(jnp.int32, (16, 256), 1) // 16
    )
    barrier = pltpu.get_barrier_semaphore()

    x, core, z, y = dp // 2, dp % 2, tk // 4, tk % 4
    zs, ys = [(z + i) % 4 for i in range(4)], [(y + i) % 4 for i in range(4)]
    experts = [((x + p // 2) % 4) * 2 + (core + p) % 2 for p in range(8)]
    givers = [experts[(8 - p // 2 * 2) % 8 + p % 2] for p in range(8)]

    def tokens(chunk, way):
        return [
            zs[way * q % 4] * 4 + (y + 4 + way * (chunk + 4 - q)) % 4
            if not isinstance(chunk, int) else zs[way * q % 4] * 4 + ys[way * (chunk - q) % 4]
            for q in range(4)
        ]

    for chunk in range(CHUNKS):
        for q, t in enumerate(tokens(chunk, 1)):
            for p, e in enumerate(experts):
                if chunk + q + p:
                    pl.semaphore_signal(barrier, inc=1, device_id=(e, t), device_id_type=MESH)

    load_ids.wait()
    for g in range(6):
        wide = jnp.concatenate([ids_ref[g]] * 16, axis=1)
        own_ids[g:g + 1, :] = jnp.sum(jnp.where(diagonal, wide, 0), axis=0, keepdims=True)
    own_ids[6:8, :] = jnp.zeros((2, 256), jnp.int32)
    ids[0] = own_ids[...]
    own_rows = table.shape[0]
    low_row = lax.broadcasted_iota(jnp.int32, (256, 256), 0).astype(jnp.float32).astype(jnp.bfloat16)
    one, none = jnp.ones((), jnp.bfloat16), jnp.zeros((), jnp.bfloat16)

    def count(k):
        for g in (0, 2, 4):
            highs, rights = [], []
            for i in range(2):
                local = ids[k, g + i:g + i + 1, :] - dp * own_rows
                inside = (local >= 0) & (local < own_rows)
                high = jnp.where(inside & diagonal, local // 256, -1)
                highs.append(high.astype(jnp.float32).astype(jnp.bfloat16))
                low = jnp.where(inside, local % 256, 0).astype(jnp.float32).astype(jnp.bfloat16)
                rights.append(jnp.where(low_row == low, one, none).astype(F8))
            row = (k % 4) * 96 + g * 16
            for v in range(own_rows // 4096):
                found = []
                for high, right in zip(highs, rights):
                    lefts = jnp.concatenate(
                        [jnp.where(high == float(v * 16 + i), one, none) for i in range(16)], axis=0
                    ).astype(F8)
                    found.append(lax.dot_general(
                        lefts, right, (((1,), (1,)), ((), ())), preferred_element_type=jnp.float32
                    ))
                for i in range(16):
                    at, of = (v * 16 + i) * 256, slice(i * 16, (i + 1) * 16)
                    counts[row:row + 32, at:at + 256] = jnp.concatenate(
                        [found[0][of], found[1][of]], axis=0
                    ).astype(F8)

    def split(step, carry):
        at = pl.ds(pl.multiple_of(step * 512, 512), 512)
        rows = table[at, :].astype(jnp.float32) * 64.0
        first = rows.astype(F8)
        pair[at, :128] = first
        pair[at, 128:] = ((rows - first.astype(jnp.float32)) * 16.0).astype(F8)
        return carry

    count(0)
    load_table.wait()
    lax.fori_loop(0, own_rows // 512, split, 0)
    pl.semaphore_wait(barrier, CHUNKS * PER - 1)
    for k in range(1, 8):
        pltpu.make_async_remote_copy(
            src_ref=own_ids, dst_ref=ids.at[k], send_sem=id_send_sem.at[k - 1],
            recv_sem=id_sem.at[k - 1], device_id=(peer_of(k, dp, 1), tk), device_id_type=MESH,
        ).start()
    load_routes.wait()
    own_routes = jnp.concatenate([routes_ref[...]] * 2, axis=2)
    expert = lax.broadcasted_iota(jnp.int32, (16, 8, 32), 1)
    picks = (own_routes[:, 0:1, :] == expert) | (own_routes[:, 1:2, :] == expert)
    row = lax.broadcasted_iota(jnp.int32, (32, 32), 0)
    col = lax.broadcasted_iota(jnp.int32, (32, 32), 1)
    before = jnp.where((row // 16 == col // 16) & (row < col), 1.0, 0.0).astype(jnp.bfloat16)
    ones = jnp.where(picks, 1.0, 0.0)
    place = jnp.dot(
        ones.reshape(128, 32).astype(jnp.bfloat16), before, preferred_element_type=jnp.float32
    ).reshape(16, 8, 32)
    place = jnp.where(picks, place, -1.0)
    slot = lax.broadcasted_iota(jnp.int32, (16, 16, 32), 1)
    half = lax.broadcasted_iota(jnp.int32, (16, 16, 32), 2) // 16
    number = jnp.where(slot // 8 == half, slot % 8, -2).astype(jnp.float32)
    for e in range(8):
        slots[:, e * 16:(e + 1) * 16, :] = jnp.where(
            place[:, e:e + 1, :] == number, 1.0, 0.0
        ).astype(jnp.bfloat16)

    for part_no in range(2):
        for k in range(part_no * 4, part_no * 4 + 4):
            if k:
                pltpu.make_async_copy(ids.at[k], ids.at[k], id_sem.at[k - 1]).wait()
                count(k)
        sums[...] = jnp.zeros_like(sums)

        def pool(step, carry):
            at = pl.ds(pl.multiple_of(step * 8192, 8192), 8192)
            sums[...] += jnp.dot(counts[:, at], pair[at, :], preferred_element_type=jnp.float32)
            return carry

        lax.fori_loop(0, own_rows // 8192, pool, 0)
        pooled = ((sums[:, :128] + sums[:, 128:] * (1.0 / 16.0)) * (0.25 / 64.0)).astype(jnp.bfloat16).reshape(4, 96, 128)
        for k in range(part_no * 4, part_no * 4 + 4):
            if k == 0:
                part[0] = pooled[0]
            else:
                part_send[k] = pooled[k % 4]
                pltpu.make_async_remote_copy(
                    src_ref=part_send.at[k], dst_ref=part.at[k], send_sem=part_send_sem.at[k - 1],
                    recv_sem=part_sem.at[k - 1], device_id=(peer_of(k, dp, -1), tk),
                    device_id_type=MESH,
                ).start()
    for k in range(1, 8):
        pltpu.make_async_copy(part.at[k], part.at[k], part_sem.at[k - 1]).wait()
    cold = part[0].astype(jnp.float32)
    for k in range(1, 8):
        cold += part[k].astype(jnp.float32)
    cold = cold.astype(jnp.bfloat16)
    cold = jnp.concatenate([cold[g * 16:(g + 1) * 16] for g in range(6)], axis=1)

    load_dense.wait()
    features = [dense_ref[t] for t in range(15)] + [cold]
    for h in range(16):
        mixed = jnp.concatenate([f[:, h * 48:(h + 1) * 48] for f in features], axis=1)
        rows = layer_norm(mixed.astype(jnp.float32) + features[h].astype(jnp.float32))
        rows = rows.astype(jnp.bfloat16)
        normed[h] = rows
    for chunk in range(CHUNKS):
        for q, t in enumerate(tokens(chunk, 1)):
            rows = normed[t]
            halves = jnp.concatenate([rows[:, :384], rows[:, 384:]], axis=0)
            out = jnp.dot(slots[t], halves, preferred_element_type=jnp.float32)
            send[pl.ds(t * 8, 8)] = out.astype(jnp.bfloat16).reshape(8, 16, 384)
            for p, e in enumerate(experts):
                r = chunk * PER + q * 8 + p
                if r:
                    pltpu.make_async_remote_copy(
                        src_ref=send.at[t * 8 + e], dst_ref=recv.at[r],
                        send_sem=send_sem, recv_sem=recv_sem.at[chunk],
                        device_id=(e, t), device_id_type=MESH,
                    ).start()
    pltpu.make_async_copy(send.at[mine], recv.at[0], recv_sem.at[0]).start()
    load1.wait()
    load2.wait()
    load_router.wait()
    which = lax.broadcasted_iota(jnp.int32, (PER * CAP, 8), 1) == dp

    def work(c, carry):
        span = pl.ds(c * PER, PER)
        pltpu.make_async_copy(recv.at[span], recv.at[span], recv_sem.at[c]).wait()
        got = recv[span].astype(jnp.float32)
        rows = jnp.concatenate([got[:, :CAP], got[:, CAP:]], axis=2)
        rows = rows.reshape(PER * CAP, 768).astype(jnp.bfloat16)
        total = jnp.zeros((PER * CAP, 768), jnp.float32)
        for j in range(4):
            hidden = jnp.dot(rows, w1[:, j * 768:(j + 1) * 768], preferred_element_type=jnp.float32)
            hidden = gelu(hidden).astype(jnp.bfloat16)
            total += jnp.dot(hidden, w2[j * 768:(j + 1) * 768, :], preferred_element_type=jnp.float32)
        logits = lax.dot_general(
            rows, router_ref[tk], (((1,), (1,)), ((), ())), preferred_element_type=jnp.float32
        )
        gate = jax.nn.sigmoid(jnp.sum(jnp.where(which, logits, 0.0), axis=1, keepdims=True))
        total = (total * gate).reshape(PER, CAP, 768)
        back_send[span] = jnp.concatenate(
            [total[:, :, :384], total[:, :, 384:]], axis=1
        ).astype(jnp.bfloat16)

        for q, t in enumerate(tokens(c, -1)):
            for p, e in enumerate(givers):
                r = c * PER + q * 8 + p
                away = pltpu.make_async_remote_copy(
                    src_ref=back_send.at[r], dst_ref=back.at[mine],
                    send_sem=back_send_sem, recv_sem=back_sem.at[c],
                    device_id=(e, t), device_id_type=MESH,
                )
                if q + p:
                    away.start()
                else:
                    pl.when(c > 0)(away.start)

        @pl.when(c == 0)
        def _():
            pltpu.make_async_copy(back_send.at[0], back.at[mine], back_sem.at[0]).start()

        return carry

    lax.fori_loop(0, CHUNKS, work, 0)

    def finish(c, carry):
        span = pl.ds(c * PER, PER)
        pltpu.make_async_copy(back.at[span], back.at[span], back_sem.at[c]).wait()
        for t in tokens(c, 1):
            answers = back[pl.ds(t * 8, 8)].reshape(128, 384)
            moe = lax.dot_general(
                slots[t], answers, (((0,), (0,)), ((), ())), preferred_element_type=jnp.float32
            )
            moe = jnp.concatenate([moe[:16], moe[16:]], axis=1)
            out_ref[t] = layer_norm(normed[t].astype(jnp.float32) + moe).astype(jnp.bfloat16)
        return carry

    lax.fori_loop(0, CHUNKS, finish, 0)
    for k in range(1, 8):
        pltpu.make_async_copy(own_ids, own_ids, id_send_sem.at[k - 1]).wait()
        pltpu.make_async_copy(part_send.at[k], part_send.at[k], part_send_sem.at[k - 1]).wait()
    sent = pl.ds(1, CHUNKS * PER - 1)
    pltpu.make_async_copy(send.at[sent], send.at[sent], send_sem).wait()
    pltpu.make_async_copy(back_send.at[sent], back_send.at[sent], back_send_sem).wait()


def run_block(dense, ids, routes, router, table, w_in, w_out):
    vmem = pl.BlockSpec(memory_space=pltpu.VMEM)
    return pl.pallas_call(
        block_kernel,
        out_shape=jax.ShapeDtypeStruct((16, 16, 768), jnp.bfloat16),
        in_specs=[pl.BlockSpec(memory_space=pltpu.HBM)] * 7,
        out_specs=vmem,
        scratch_shapes=[
            pltpu.VMEM(dense.shape, jnp.bfloat16),
            pltpu.VMEM(ids.shape, jnp.int32),
            pltpu.VMEM(routes.shape, jnp.int32),
            pltpu.VMEM(router.shape, jnp.bfloat16),
            pltpu.VMEM((768, 3072), jnp.bfloat16),
            pltpu.VMEM((3072, 768), jnp.bfloat16),
        ]
        + [pltpu.VMEM((128, 16, 384), jnp.bfloat16)] * 4
        + [
            pltpu.VMEM((16, 128, 32), jnp.bfloat16),
            pltpu.VMEM((16, 16, 768), jnp.bfloat16),
            pltpu.VMEM(table.shape, jnp.bfloat16),
            pltpu.VMEM((table.shape[0], 256), F8),
            pltpu.VMEM((8, 256), jnp.int32),
            pltpu.VMEM((8, 8, 256), jnp.int32),
            pltpu.VMEM((384, table.shape[0]), F8),
            pltpu.VMEM((384, 256), jnp.float32),
            pltpu.VMEM((8, 96, 128), jnp.bfloat16),
            pltpu.VMEM((8, 96, 128), jnp.bfloat16),
            pltpu.SemaphoreType.DMA((7,)),
            pltpu.SemaphoreType.DMA,
            pltpu.SemaphoreType.DMA((CHUNKS,)),
            pltpu.SemaphoreType.DMA,
            pltpu.SemaphoreType.DMA((CHUNKS,)),
        ]
        + [pltpu.SemaphoreType.DMA((7,))] * 4,
        compiler_params=pltpu.CompilerParams(
            collective_id=0, has_side_effects=True, vmem_limit_bytes=58 * 1024 * 1024
        ),
        cost_estimate=pl.CostEstimate(
            flops=4 * 1024 * 768 * 3072, bytes_accessed=2 * 2 * 768 * 3072, transcendentals=0
        ),
    )(dense, ids, routes, router, table, w_in, w_out)


def shards(dense_tokens, cold_table, cold_ids, routes, router, w_in, w_out):
    out = run_block(
        dense_tokens.transpose(1, 0, 2),
        cold_ids.transpose(1, 0, 2),
        routes.transpose(0, 2, 1),
        router.transpose(0, 2, 1),
        cold_table,
        w_in[0, 0],
        w_out[0, 0],
    )
    return out.transpose(1, 0, 2)


def solution(mesh):
    return jax.shard_map(
        shards,
        mesh=mesh,
        in_specs=(
            P(("dp", "token"), None, None),
            P("dp", None),
            P(("dp", "token"), None, None),
            P(None, ("dp", "token"), None),
            P(),
            P("token", "dp", None, None),
            P("token", "dp", None, None),
        ),
        out_specs=P(("dp", "token"), None, None),
        check_vma=False,
    )
```

```python
import functools
import math

import jax
import jax.numpy as jnp
from jax import lax
from jax.experimental import pallas as pl
from jax.experimental.pallas import tpu as pltpu
from jax.sharding import PartitionSpec as P

CHUNKS = 4
PER = 32
CAP = 8
F8 = jnp.float8_e4m3fn
MESH = pl.DeviceIdType.MESH


def peer_of(k, dp, way):
    return ((dp // 2 + 4 + way * (k // 2)) % 4) * 2 + (dp % 2 + k) % 2


def layer_norm(value):
    mean = jnp.mean(value, axis=-1, keepdims=True)
    centred = value - mean
    var = jnp.mean(centred * centred, axis=-1, keepdims=True)
    return centred * lax.rsqrt(var + 1e-05)


def gelu(value):
    return 0.5 * value * (1.0 + lax.erf(value * math.sqrt(0.5)))


def block_kernel(
    dense_hbm, ids_hbm, routes_hbm, router_hbm, table_hbm, w1_hbm, w2_hbm, out_ref,
    dense_ref, ids_ref, routes_ref, router_ref, w1, w2, send, recv, back_send, back, slots, normed,
    table, pair, own_ids, ids, counts, sums, part_send, part, early,
    w_sem, send_sem, recv_sem, back_send_sem, back_sem, id_send_sem, id_sem, part_send_sem, part_sem,
):
    dp, tk = lax.axis_index("dp"), lax.axis_index("token")
    mine = tk * 8 + dp
    load_ids = pltpu.make_async_copy(ids_hbm, ids_ref, w_sem.at[3])
    load_routes = pltpu.make_async_copy(routes_hbm, routes_ref, w_sem.at[4])
    load_dense = pltpu.make_async_copy(dense_hbm, dense_ref, w_sem.at[5])
    load_router = pltpu.make_async_copy(router_hbm, router_ref, w_sem.at[6])
    load_ids.start()
    load_routes.start()
    load_dense.start()
    load_router.start()
    load_table = pltpu.make_async_copy(table_hbm, table, w_sem.at[2])
    load_table.start()
    load1 = pltpu.make_async_copy(w1_hbm, w1, w_sem.at[0])
    load2 = pltpu.make_async_copy(w2_hbm, w2, w_sem.at[1])
    load1.start()
    load2.start()
    diagonal = (
        lax.broadcasted_iota(jnp.int32, (16, 256), 0)
        == lax.broadcasted_iota(jnp.int32, (16, 256), 1) // 16
    )
    barrier = pltpu.get_barrier_semaphore()

    x, core, z, y = dp // 2, dp % 2, tk // 4, tk % 4
    zs, ys = [(z + i) % 4 for i in range(4)], [(y + i) % 4 for i in range(4)]
    experts = [((x + p // 2) % 4) * 2 + (core + p) % 2 for p in range(8)]
    givers = [experts[(8 - p // 2 * 2) % 8 + p % 2] for p in range(8)]

    def tokens(chunk, way):
        return [
            zs[way * q % 4] * 4 + (y + 4 + way * (chunk + 4 - q)) % 4
            if not isinstance(chunk, int) else zs[way * q % 4] * 4 + ys[way * (chunk - q) % 4]
            for q in range(4)
        ]

    for chunk in range(CHUNKS):
        for q, t in enumerate(tokens(chunk, 1)):
            for p, e in enumerate(experts):
                if chunk + q + p:
                    pl.semaphore_signal(barrier, inc=1, device_id=(e, t), device_id_type=MESH)

    load_ids.wait()
    for g in range(6):
        wide = jnp.concatenate([ids_ref[g]] * 16, axis=1)
        own_ids[g:g + 1, :] = jnp.sum(jnp.where(diagonal, wide, 0), axis=0, keepdims=True)
    own_ids[6:8, :] = jnp.zeros((2, 256), jnp.int32)
    ids[0] = own_ids[...]
    own_rows = table.shape[0]
    low_row = lax.broadcasted_iota(jnp.int32, (256, 256), 0).astype(jnp.float32).astype(jnp.bfloat16)
    one, none = jnp.ones((), jnp.bfloat16), jnp.zeros((), jnp.bfloat16)

    def count(k):
        for g in (0, 2, 4):
            highs, rights = [], []
            for i in range(2):
                local = ids[k, g + i:g + i + 1, :] - dp * own_rows
                inside = (local >= 0) & (local < own_rows)
                high = jnp.where(inside & diagonal, local // 256, -1)
                highs.append(high.astype(jnp.float32).astype(jnp.bfloat16))
                low = jnp.where(inside, local % 256, 0).astype(jnp.float32).astype(jnp.bfloat16)
                rights.append(jnp.where(low_row == low, one, none).astype(F8))
            row = (k % 4) * 96 + g * 16
            for v in range(own_rows // 4096):
                found = []
                for high, right in zip(highs, rights):
                    lefts = jnp.concatenate(
                        [jnp.where(high == float(v * 16 + i), one, none) for i in range(16)], axis=0
                    ).astype(F8)
                    found.append(lax.dot_general(
                        lefts, right, (((1,), (1,)), ((), ())), preferred_element_type=jnp.float32
                    ))
                for i in range(16):
                    at, of = (v * 16 + i) * 256, slice(i * 16, (i + 1) * 16)
                    counts[row:row + 32, at:at + 256] = jnp.concatenate(
                        [found[0][of], found[1][of]], axis=0
                    ).astype(F8)

    def split(step, carry):
        at = pl.ds(pl.multiple_of(step * 512, 512), 512)
        rows = table[at, :].astype(jnp.float32) * 64.0
        first = rows.astype(F8)
        pair[at, :128] = first
        pair[at, 128:] = ((rows - first.astype(jnp.float32)) * 16.0).astype(F8)
        return carry

    count(0)
    load_table.wait()
    lax.fori_loop(0, own_rows // 512, split, 0)
    pl.semaphore_wait(barrier, CHUNKS * PER - 1)
    for k in range(1, 8):
        pltpu.make_async_remote_copy(
            src_ref=own_ids, dst_ref=ids.at[k], send_sem=id_send_sem.at[k - 1],
            recv_sem=id_sem.at[k - 1], device_id=(peer_of(k, dp, 1), tk), device_id_type=MESH,
        ).start()
    load_routes.wait()
    own_routes = jnp.concatenate([routes_ref[...]] * 2, axis=2)
    expert = lax.broadcasted_iota(jnp.int32, (16, 8, 32), 1)
    picks = (own_routes[:, 0:1, :] == expert) | (own_routes[:, 1:2, :] == expert)
    row = lax.broadcasted_iota(jnp.int32, (32, 32), 0)
    col = lax.broadcasted_iota(jnp.int32, (32, 32), 1)
    before = jnp.where((row // 16 == col // 16) & (row < col), 1.0, 0.0).astype(jnp.bfloat16)
    ones = jnp.where(picks, 1.0, 0.0)
    place = jnp.dot(
        ones.reshape(128, 32).astype(jnp.bfloat16), before, preferred_element_type=jnp.float32
    ).reshape(16, 8, 32)
    place = jnp.where(picks, place, -1.0)
    slot = lax.broadcasted_iota(jnp.int32, (16, 16, 32), 1)
    half = lax.broadcasted_iota(jnp.int32, (16, 16, 32), 2) // 16
    number = jnp.where(slot // 8 == half, slot % 8, -2).astype(jnp.float32)
    for e in range(8):
        slots[:, e * 16:(e + 1) * 16, :] = jnp.where(
            place[:, e:e + 1, :] == number, 1.0, 0.0
        ).astype(jnp.bfloat16)

    for part_no in range(2):
        for k in range(part_no * 4, part_no * 4 + 4):
            if k:
                pltpu.make_async_copy(ids.at[k], ids.at[k], id_sem.at[k - 1]).wait()
                count(k)
        sums[...] = jnp.zeros_like(sums)

        def pool(step, carry):
            at = pl.ds(pl.multiple_of(step * 8192, 8192), 8192)
            sums[...] += jnp.dot(counts[:, at], pair[at, :], preferred_element_type=jnp.float32)
            return carry

        lax.fori_loop(0, own_rows // 8192, pool, 0)
        pooled = ((sums[:, :128] + sums[:, 128:] * (1.0 / 16.0)) * (0.25 / 64.0)).astype(jnp.bfloat16).reshape(4, 96, 128)
        for k in range(part_no * 4, part_no * 4 + 4):
            if k == 0:
                part[0] = pooled[0]
            else:
                part_send[k] = pooled[k % 4]
                pltpu.make_async_remote_copy(
                    src_ref=part_send.at[k], dst_ref=part.at[k], send_sem=part_send_sem.at[k - 1],
                    recv_sem=part_sem.at[k - 1], device_id=(peer_of(k, dp, -1), tk),
                    device_id_type=MESH,
                ).start()
    load_dense.wait()
    features = [dense_ref[t] for t in range(15)] + [jnp.zeros((16, 768), jnp.bfloat16)]
    for h in range(16):
        mixed = jnp.concatenate([f[:, h * 48:(h + 1) * 48] for f in features], axis=1)
        early[h] = mixed.astype(jnp.float32) + features[h].astype(jnp.float32)
    for k in range(1, 8):
        pltpu.make_async_copy(part.at[k], part.at[k], part_sem.at[k - 1]).wait()
    cold = part[0].astype(jnp.float32)
    for k in range(1, 8):
        cold += part[k].astype(jnp.float32)
    cold = cold.astype(jnp.bfloat16)
    cold = jnp.concatenate([cold[g * 16:(g + 1) * 16] for g in range(6)], axis=1)

    gap = jnp.zeros((16, 720), jnp.bfloat16)
    for h in range(16):
        late = jnp.concatenate([gap, cold[:, h * 48:(h + 1) * 48]], axis=1).astype(jnp.float32)
        rows = early[h] + (late if h < 15 else late + cold.astype(jnp.float32))
        rows = layer_norm(rows).astype(jnp.bfloat16)
        normed[h] = rows
    for chunk in range(CHUNKS):
        for q, t in enumerate(tokens(chunk, 1)):
            rows = normed[t]
            halves = jnp.concatenate([rows[:, :384], rows[:, 384:]], axis=0)
            out = jnp.dot(slots[t], halves, preferred_element_type=jnp.float32)
            send[pl.ds(t * 8, 8)] = out.astype(jnp.bfloat16).reshape(8, 16, 384)
            for p in (4, 5, 2, 3, 6, 7, 0, 1):
                e = experts[p]
                r = chunk * PER + q * 8 + p
                if r:
                    pltpu.make_async_remote_copy(
                        src_ref=send.at[t * 8 + e], dst_ref=recv.at[r],
                        send_sem=send_sem, recv_sem=recv_sem.at[chunk],
                        device_id=(e, t), device_id_type=MESH,
                    ).start()
    pltpu.make_async_copy(send.at[mine], recv.at[0], recv_sem.at[0]).start()
    load1.wait()
    load2.wait()
    load_router.wait()
    which = lax.broadcasted_iota(jnp.int32, (PER * CAP, 8), 1) == dp

    def work(c, carry):
        span = pl.ds(c * PER, PER)
        pltpu.make_async_copy(recv.at[span], recv.at[span], recv_sem.at[c]).wait()
        got = recv[span].astype(jnp.float32)
        rows = jnp.concatenate([got[:, :CAP], got[:, CAP:]], axis=2)
        rows = rows.reshape(PER * CAP, 768).astype(jnp.bfloat16)
        total = jnp.zeros((PER * CAP, 768), jnp.float32)
        for j in range(4):
            hidden = jnp.dot(rows, w1[:, j * 768:(j + 1) * 768], preferred_element_type=jnp.float32)
            hidden = gelu(hidden).astype(jnp.bfloat16)
            total += jnp.dot(hidden, w2[j * 768:(j + 1) * 768, :], preferred_element_type=jnp.float32)
        logits = lax.dot_general(
            rows, router_ref[tk], (((1,), (1,)), ((), ())), preferred_element_type=jnp.float32
        )
        gate = jax.nn.sigmoid(jnp.sum(jnp.where(which, logits, 0.0), axis=1, keepdims=True))
        total = (total * gate).reshape(PER, CAP, 768)
        back_send[span] = jnp.concatenate(
            [total[:, :, :384], total[:, :, 384:]], axis=1
        ).astype(jnp.bfloat16)

        for q, t in enumerate(tokens(c, -1)):
            for p in (4, 5, 2, 3, 6, 7, 0, 1):
                e = givers[p]
                r = c * PER + q * 8 + p
                away = pltpu.make_async_remote_copy(
                    src_ref=back_send.at[r], dst_ref=back.at[mine],
                    send_sem=back_send_sem, recv_sem=back_sem.at[c],
                    device_id=(e, t), device_id_type=MESH,
                )
                if q + p:
                    away.start()
                else:
                    pl.when(c > 0)(away.start)

        @pl.when(c == 0)
        def _():
            pltpu.make_async_copy(back_send.at[0], back.at[mine], back_sem.at[0]).start()

        return carry

    lax.fori_loop(0, CHUNKS, work, 0)

    def finish(c, carry):
        span = pl.ds(c * PER, PER)
        pltpu.make_async_copy(back.at[span], back.at[span], back_sem.at[c]).wait()
        for t in tokens(c, 1):
            answers = back[pl.ds(t * 8, 8)].reshape(128, 384)
            moe = lax.dot_general(
                slots[t], answers, (((0,), (0,)), ((), ())), preferred_element_type=jnp.float32
            )
            moe = jnp.concatenate([moe[:16], moe[16:]], axis=1)
            out_ref[t] = layer_norm(normed[t].astype(jnp.float32) + moe).astype(jnp.bfloat16)
        return carry

    lax.fori_loop(0, CHUNKS, finish, 0)
    for k in range(1, 8):
        pltpu.make_async_copy(own_ids, own_ids, id_send_sem.at[k - 1]).wait()
        pltpu.make_async_copy(part_send.at[k], part_send.at[k], part_send_sem.at[k - 1]).wait()
    sent = pl.ds(1, CHUNKS * PER - 1)
    pltpu.make_async_copy(send.at[sent], send.at[sent], send_sem).wait()
    pltpu.make_async_copy(back_send.at[sent], back_send.at[sent], back_send_sem).wait()


def run_block(dense, ids, routes, router, table, w_in, w_out):
    vmem = pl.BlockSpec(memory_space=pltpu.VMEM)
    return pl.pallas_call(
        block_kernel,
        out_shape=jax.ShapeDtypeStruct((16, 16, 768), jnp.bfloat16),
        in_specs=[pl.BlockSpec(memory_space=pltpu.HBM)] * 7,
        out_specs=vmem,
        scratch_shapes=[
            pltpu.VMEM(dense.shape, jnp.bfloat16),
            pltpu.VMEM(ids.shape, jnp.int32),
            pltpu.VMEM(routes.shape, jnp.int32),
            pltpu.VMEM(router.shape, jnp.bfloat16),
            pltpu.VMEM((768, 3072), jnp.bfloat16),
            pltpu.VMEM((3072, 768), jnp.bfloat16),
        ]
        + [pltpu.VMEM((128, 16, 384), jnp.bfloat16)] * 4
        + [
            pltpu.VMEM((16, 128, 32), jnp.bfloat16),
            pltpu.VMEM((16, 16, 768), jnp.bfloat16),
            pltpu.VMEM(table.shape, jnp.bfloat16),
            pltpu.VMEM((table.shape[0], 256), F8),
            pltpu.VMEM((8, 256), jnp.int32),
            pltpu.VMEM((8, 8, 256), jnp.int32),
            pltpu.VMEM((384, table.shape[0]), F8),
            pltpu.VMEM((384, 256), jnp.float32),
            pltpu.VMEM((8, 96, 128), jnp.bfloat16),
            pltpu.VMEM((8, 96, 128), jnp.bfloat16),
            pltpu.VMEM((16, 16, 768), jnp.float32),
            pltpu.SemaphoreType.DMA((7,)),
            pltpu.SemaphoreType.DMA,
            pltpu.SemaphoreType.DMA((CHUNKS,)),
            pltpu.SemaphoreType.DMA,
            pltpu.SemaphoreType.DMA((CHUNKS,)),
        ]
        + [pltpu.SemaphoreType.DMA((7,))] * 4,
        compiler_params=pltpu.CompilerParams(
            collective_id=0, has_side_effects=True, vmem_limit_bytes=58 * 1024 * 1024
        ),
        cost_estimate=pl.CostEstimate(
            flops=4 * 1024 * 768 * 3072, bytes_accessed=2 * 2 * 768 * 3072, transcendentals=0
        ),
    )(dense, ids, routes, router, table, w_in, w_out)


def shards(dense_tokens, cold_table, cold_ids, routes, router, w_in, w_out):
    out = run_block(
        dense_tokens.transpose(1, 0, 2),
        cold_ids.transpose(1, 0, 2),
        routes.transpose(0, 2, 1),
        router.transpose(0, 2, 1),
        cold_table,
        w_in[0, 0],
        w_out[0, 0],
    )
    return out.transpose(1, 0, 2)


def solution(mesh):
    return jax.shard_map(
        shards,
        mesh=mesh,
        in_specs=(
            P(("dp", "token"), None, None),
            P("dp", None),
            P(("dp", "token"), None, None),
            P(None, ("dp", "token"), None),
            P(),
            P("token", "dp", None, None),
            P("token", "dp", None, None),
        ),
        out_specs=P(("dp", "token"), None, None),
        check_vma=False,
    )
```
